32 devices in a mesh: gx: 8 (over y, x, core), gy: 4 (over z).
Axes of the slice: x: 2, y: 2, z: 4, core: 2. Of those that a mesh axis runs over, the one named last changes fastest.
Arguments:
- velocity: float32 [64, 32, 128], P('gx', 'gy'), may hold values from -6 to 6
- cotangent: float32 [64, 32, 128], P('gx', 'gy'), may hold values from -6 to 6
- block_ids: int32 [8, 4, 128], P('gx', 'gy'), may hold values from 0 to 127, as said below
- fluid_count: int32 [8, 4], P('gx', 'gy'), may hold values from 32 to 128, as said below
- fluid_cells: int32 [8, 4, 8192], P('gx', 'gy'), may hold values 0 or 1
- w_in: bfloat16 [64, 7], replicated, may hold values from -2 to 2
- w_mid: bfloat16 [64, 64], replicated, may hold values from -0.75 to 0.75
- w_out: bfloat16 [1, 64], replicated, may hold values from -0.75 to 0.75
Outputs:
- new_field: float32 [64, 32, 128], P('gx', 'gy')
- grad_field: float32 [64, 32, 128], P('gx', 'gy')
- grad_in: float32 [64, 7], replicated
- grad_mid: float32 [64, 64], replicated
- grad_out: float32 [1, 64], replicated
The draws below stay inside these ranges and needn't reach their ends.
Inputs may be any that keep to these rules, and one draw needn't show every extreme that they name: `block_ids`: within one device's list the block numbers are distinct. `fluid_count`: some device's list is wholly live.
All inputs are finite; a program needn't handle non-finite values. No bound on the sum of `fluid_cells` on one device may be relied on, other than what follows from the above.
Results may differ from the reference program's by a relative error of at most 0.018.
Values sent between devices are 32-bit elements; how exact they have to be, the bound alone decides.
A program may use at most 64 MiB of HBM per device.

```python
import jax
import jax.numpy as jnp
from jax import lax

CX = 8
CY = 8
NZ = 128
BCAP = 128
CH = 64
NB = 128
NX = 64
NY = 32
N_GX = 8
N_GY = 4


def draw_block_ids(key, part):
    groups = NX // CX * (NY // CY)
    subkeys = jax.random.split(key, groups)

    def pick(subkey):
        return jax.random.permutation(subkey, NB)[:BCAP]
    chosen = jax.vmap(pick)(subkeys)
    return chosen.reshape(NX // CX, NY // CY, BCAP).astype(jnp.int32)


def draw_fluid_count(key, part):
    groups = NX // CX * (NY // CY)
    counts = jax.random.randint(jax.random.fold_in(key, 11), (groups,), max(1, BCAP // 4), BCAP + 1)
    fullest = jax.random.randint(jax.random.fold_in(key, 12), (), 0, groups)
    counts = jnp.where(jnp.arange(groups) == fullest, BCAP, counts)
    return counts.reshape(NX // CX, NY // CY).astype(jnp.int32)


def plant(entries, own_key, low, top_value):
    place = [jax.random.randint(jax.random.fold_in(own_key, axis), (), 0, length) for axis, length in enumerate(entries.shape)]
    main_axis = entries.shape.index(max(entries.shape))
    next_to = place[:main_axis] + [(place[main_axis] + 1) % entries.shape[main_axis]] + place[main_axis + 1:]
    return entries.at[tuple(place)].set(low).at[tuple(next_to)].set(top_value)


def steps_of(own_key, shape, cuts, least, top_value):
    def one(position, blocks):
        steps = jax.random.uniform(jax.random.fold_in(jax.random.fold_in(own_key, 6), position), (blocks,), jnp.float32, least / len(cuts), top_value / len(cuts))
        return jnp.repeat(jnp.exp(steps), shape[position] // blocks).reshape((-1,) + (1,) * (len(shape) - position - 1))

    factor_of = one(*cuts[0])
    for cut in cuts[1:]:
        factor_of = factor_of * one(*cut)
    return factor_of


def centred(rng, shape, width, most, shards=(), kind=jnp.bfloat16):
    level = steps_of(rng, shape, shards, -0.22, 0.18) if shards else 1.0
    entries = jax.random.normal(rng, shape, jnp.float32) * width * level
    return jnp.minimum(jnp.maximum(entries, -most), most).astype(kind)


def setup_inputs(seed: int = 0) -> dict:
    keys = jax.random.split(jax.random.key(seed), 9)
    velocity = centred(keys[0], (NX, NY, NZ), 1.0, 6.0, ((0, 8), (1, 4)), jnp.float32)
    cotangent = centred(keys[1], (NX, NY, NZ), 1.0, 6.0, ((0, 8), (1, 4)), jnp.float32)
    block_ids = draw_block_ids(jax.random.fold_in(keys[8], 71), 0)
    fluid_count = draw_fluid_count(jax.random.fold_in(keys[8], 71), 0)
    fluid_cells = plant((jax.random.randint(keys[4], (NX // CX, NY // CY, BCAP * 64), 0, 4) < 3).astype(jnp.int32), jax.random.fold_in(keys[4], 1), 0, 1)
    w_in = centred(keys[5], (CH, 7), 7 ** -0.5, 2.0)
    w_mid = centred(keys[6], (CH, CH), CH ** -0.5, 0.75)
    w_out = centred(keys[7], (1, CH), CH ** -0.5, 0.75)
    return {"velocity": velocity, "cotangent": cotangent, "block_ids": block_ids, "fluid_count": fluid_count, "fluid_cells": fluid_cells, "w_in": w_in, "w_mid": w_mid, "w_out": w_out}


viscosity = 0.1

def to_blocks(field):
    lead = field.shape[:-3]
    sizex, sizey, sizez = field.shape[-3:]
    count = len(lead)
    shaped = field.reshape(lead + (sizex // 4, 4, sizey // 4, 4, sizez // 4, 4))
    order = list(range(count)) + [count, count + 2, count + 4, count + 1, count + 3, count + 5]
    return shaped.transpose(order).reshape(lead + (sizex * sizey * sizez // 64, 64))

def from_blocks(blocks, sizex, sizey, sizez):
    lead = blocks.shape[:-2]
    count = len(lead)
    shaped = blocks.reshape(lead + (sizex // 4, sizey // 4, sizez // 4, 4, 4, 4))
    order = list(range(count)) + [count, count + 3, count + 1, count + 4, count + 2, count + 5]
    return shaped.transpose(order).reshape(lead + (sizex, sizey, sizez))

def closure_tile(padded, cotile, ids, count, fluid, w_in, w_mid, w_out):
    sizex = padded.shape[0] - 2
    sizey = padded.shape[1] - 2
    sizez = padded.shape[2]
    slots = ids.shape[0]
    nblocks = sizex * sizey * sizez // 64
    center = padded[1:-1, 1:-1]
    stencil = jnp.stack([center, padded[2:, 1:-1], padded[:-2, 1:-1], padded[1:-1, 2:], padded[1:-1, :-2], jnp.roll(center, -1, 2), jnp.roll(center, 1, 2)]).astype(jnp.bfloat16)
    chosen = jnp.take(to_blocks(stencil), ids, axis=1).reshape(7, slots * 64)
    live = (jnp.arange(slots) < count).astype(jnp.float32)
    weight = (fluid.reshape(slots, 64).astype(jnp.float32) * live[:, None]).reshape(slots * 64)
    h1 = jnp.tanh(jnp.dot(w_in, chosen, preferred_element_type=jnp.float32)).astype(jnp.bfloat16)
    h2 = jnp.tanh(jnp.dot(w_mid, h1, preferred_element_type=jnp.float32)).astype(jnp.bfloat16)
    closure = jnp.dot(w_out, h2, preferred_element_type=jnp.float32)[0] * weight
    corr_blocks = jnp.zeros((nblocks, 64), jnp.float32).at[ids].add(closure.reshape(slots, 64))
    corr = from_blocks(corr_blocks, sizex, sizey, sizez)
    cot_sel = jnp.take(to_blocks(cotile), ids, axis=0).reshape(slots * 64)
    dcl = (cot_sel * weight).astype(jnp.bfloat16)
    h2f = h2.astype(jnp.float32)
    h1f = h1.astype(jnp.float32)
    dh2 = jnp.dot(w_out.T, dcl[None, :], preferred_element_type=jnp.float32)
    da2 = (dh2 * (1.0 - h2f * h2f)).astype(jnp.bfloat16)
    dh1 = jnp.dot(w_mid.T, da2, preferred_element_type=jnp.float32)
    da1 = (dh1 * (1.0 - h1f * h1f)).astype(jnp.bfloat16)
    dfeat = jnp.dot(w_in.T, da1, preferred_element_type=jnp.float32)
    dims = (((1,), (1,)), ((), ()))
    gin = lax.dot_general(da1, chosen, dims, preferred_element_type=jnp.float32)
    gmid = lax.dot_general(da2, h1, dims, preferred_element_type=jnp.float32)
    gout = lax.dot_general(dcl[None, :], h2, dims, preferred_element_type=jnp.float32)
    dense = jnp.zeros((7, nblocks, 64), jnp.float32).at[:, ids].add(dfeat.reshape(7, slots, 64))
    dense = from_blocks(dense, sizex, sizey, sizez)
    local = dense[0] + jnp.roll(dense[5], 1, 2) + jnp.roll(dense[6], -1, 2)
    return (corr, local, dense[1:5], gin, gmid, gout)

def laplace(field):
    total = jnp.roll(field, -1, 0) + jnp.roll(field, 1, 0) + jnp.roll(field, -1, 1)
    total = total + jnp.roll(field, 1, 1) + jnp.roll(field, -1, 2) + jnp.roll(field, 1, 2)
    return total - 6.0 * field

def untile(tiles):
    return tiles.reshape(N_GX, N_GY, CX, CY, NZ).transpose(0, 2, 1, 3, 4).reshape(NX, NY, NZ)

def reference(velocity, cotangent, block_ids, fluid_count, fluid_cells, w_in, w_mid, w_out):
    wrapped = jnp.pad(velocity, ((1, 1), (1, 1), (0, 0)), mode='wrap')

    def one_tile(index):
        row = index // N_GY
        col = index % N_GY
        zero = jnp.zeros((), jnp.int32)
        padded = lax.dynamic_slice(wrapped, (row * CX, col * CY, zero), (CX + 2, CY + 2, NZ))
        cotile = lax.dynamic_slice(cotangent, (row * CX, col * CY, zero), (CX, CY, NZ))
        return closure_tile(padded, cotile, block_ids[row, col], fluid_count[row, col], fluid_cells[row, col], w_in, w_mid, w_out)
    corr, local, side, gin, gmid, gout = lax.map(one_tile, jnp.arange(N_GX * N_GY, dtype=jnp.int32))
    new_field = velocity + viscosity * laplace(velocity) + untile(corr)
    grad_field = cotangent + viscosity * laplace(cotangent) + untile(local)
    grad_field = grad_field + jnp.roll(untile(side[:, 0]), 1, 0) + jnp.roll(untile(side[:, 1]), -1, 0)
    grad_field = grad_field + jnp.roll(untile(side[:, 2]), 1, 1) + jnp.roll(untile(side[:, 3]), -1, 1)
    scale = 1.0 / jnp.sqrt(jnp.float32(N_GX * N_GY * BCAP * 64))
    return (new_field, grad_field, lax.optimization_barrier(jnp.sum(gin, 0)) * scale, lax.optimization_barrier(jnp.sum(gmid, 0)) * scale, lax.optimization_barrier(jnp.sum(gout, 0)) * scale)
```

```python
import functools

import jax
import jax.numpy as jnp
from jax import lax
from jax.experimental import pallas as pl
from jax.experimental.pallas import tpu as pltpu
from jax.sharding import PartitionSpec as P

viscosity = 0.1
MESH = pl.DeviceIdType.MESH
BF = jnp.bfloat16
F32 = jnp.float32


def iota(shape, dim):
    return lax.broadcasted_iota(jnp.int32, shape, dim)


def dot(a, b):
    return jnp.dot(a, b, preferred_element_type=F32)


def dot_nt(a, b):
    return lax.dot_general(a, b, (((1,), (1,)), ((), ())), preferred_element_type=F32)


def ones_where(mask):
    return jnp.where(mask, 1.0, 0.0).astype(BF)


def fluid_field(ids, count, fluid2):
    half, lanes = fluid2.shape
    cells = lanes // 2
    slots = ids.shape[1]
    lane = iota((1, slots), 1)
    live = jnp.where(lane < count, ids, -1).astype(F32)
    spread = jnp.broadcast_to(live, (half, slots))
    slot_of = iota((half, slots), 1)
    row = iota((half, slots), 0)
    fluid_t = jnp.transpose(fluid2.astype(F32)).astype(BF)
    block = iota((half, 512), 1) // 4
    placed = None
    for h in range(2):
        col = jnp.sum(jnp.where(slot_of == 2 * row + h, spread, 0.0), axis=1, keepdims=True)
        hot = ones_where(jnp.broadcast_to(col, (half, 512)) == block.astype(F32))
        part = dot(fluid_t[h * cells : (h + 1) * cells], hot)
        placed = part if placed is None else placed + part
    keep = (iota((cells, 512), 0) % 4) == (iota((cells, 512), 1) % 4)
    placed = jnp.where(keep, placed, 0.0).astype(BF)
    rhs = jnp.concatenate(
        [
            jnp.concatenate([placed[:, 0:128], placed[:, 256:384]], axis=1),
            jnp.concatenate([placed[:, 128:256], placed[:, 384:512]], axis=1),
        ],
        axis=0,
    )
    r = iota((32, 2 * cells), 0)
    c = iota((32, 2 * cells), 1)
    pick = (r // 8 == (c % 64) // 16) & ((r % 8) // 4 == c // 64) & (r % 4 == (c % 16) // 4)
    return dot(ones_where(pick), rhs)


def kernel(
    n, m, v_ref, c_ref, ids_ref, count_ref, fluid_ref, win_ref, wmid_ref, wout_ref,
    new_ref, grad_ref, tot_ref,
    hsend, hrecv, ssend, srecv, parts, rsbuf, gybuf, agbuf,
    hs_sem, hr_sem, ss_sem, sr_sem, rs_ssem, rs_rsem, gy_ssem, gy_rsem, ag_ssem, ag_rsem,
):
    px = lax.axis_index("gx")
    py = lax.axis_index("gy")
    rows = parts.shape[1]

    barrier = pltpu.get_barrier_semaphore()
    for d in range(1, n):
        pl.semaphore_signal(barrier, inc=1, device_id=(lax.rem(px + d, n), py), device_id_type=MESH)
    for d in range(1, m):
        pl.semaphore_signal(barrier, inc=1, device_id=(px, lax.rem(py + d, m)), device_id_type=MESH)

    v = v_ref[...]
    cot = c_ref[...]
    for f, field in enumerate((v, cot)):
        hsend[0, f] = field[0]
        hsend[1, f] = field[7]
        hsend[2, f] = field[:, 0, :]
        hsend[3, f] = field[:, 7, :]
    near = (
        (lax.rem(px + n - 1, n), py),
        (lax.rem(px + 1, n), py),
        (px, lax.rem(py + m - 1, m)),
        (px, lax.rem(py + 1, m)),
    )
    pl.semaphore_wait(barrier, n + m - 2)
    halo = [
        pltpu.make_async_remote_copy(
            src_ref=hsend.at[k], dst_ref=hrecv.at[k], send_sem=hs_sem.at[k], recv_sem=hr_sem.at[k],
            device_id=near[k], device_id_type=MESH,
        )
        for k in range(4)
    ]
    for copy in halo:
        copy.start()

    weight = fluid_field(ids_ref[...], count_ref[...], fluid_ref[...])
    win = win_ref[...]
    wmid = wmid_ref[...]
    wout = wout_ref[...]
    eye = ones_where(iota((64, 64), 0) == iota((64, 64), 1))
    wmid_t = dot_nt(eye, wmid).astype(BF)
    widen = ones_where(iota((7, 56), 0) == iota((7, 56), 1) // 8)
    win_y = dot(win, widen)
    tall = jnp.concatenate([win_y] * 8, axis=0)
    win_big = jnp.where(iota((512, 56), 0) // 64 == iota((512, 56), 1) % 8, tall, 0.0).astype(BF)
    repeat = ones_where(iota((64, 512), 0) == iota((64, 512), 1) % 64)
    widen_t = ones_where(iota((56, 7), 1) == iota((56, 7), 0) // 8)
    win_t = dot(dot_nt(widen_t, win).astype(BF), repeat)
    same_y = iota((56, 512), 0) % 8 == iota((56, 512), 1) // 64
    win_tbig = jnp.where(same_y, win_t, 0.0).astype(BF)
    wout_row = jnp.broadcast_to(dot(wout, repeat), (8, 512))
    wout_big = jnp.where(iota((8, 512), 0) == iota((8, 512), 1) // 64, wout_row, 0.0).astype(BF)
    wout_col = jnp.concatenate([dot_nt(eye, jnp.broadcast_to(wout, (8, 64)))] * 8, axis=0)
    wout_tbig = jnp.where(iota((512, 8), 0) // 64 == iota((512, 8), 1), wout_col, 0.0).astype(BF)

    row = iota((8, 128), 0)
    zup = [pltpu.roll(v[x], 127, 1) for x in range(8)]
    zdn = [pltpu.roll(v[x], 1, 1) for x in range(8)]

    for copy in halo:
        copy.wait()

    def beside(field, f, x):
        up = field[x + 1] if x < 7 else hrecv[0, f]
        down = field[x - 1] if x > 0 else hrecv[1, f]
        north = jnp.where(row == 7, hrecv[2, f, x : x + 1, :], pltpu.roll(field[x], 7, 0))
        south = jnp.where(row == 0, hrecv[3, f, x : x + 1, :], pltpu.roll(field[x], 1, 0))
        return [up, down, north, south]

    def cat_y(a):
        return jnp.concatenate([a[64 * y : 64 * y + 64] for y in range(8)], axis=1)

    def stack_y(a):
        return jnp.concatenate([a[:, 256 * y : 256 * y + 256] for y in range(8)], axis=0)

    gmid = jnp.zeros((64, 64), F32)
    gin = jnp.zeros((56, 512), F32)
    gout = jnp.zeros((8, 512), F32)
    dfs = []
    for pair in range(4):
        feats = []
        bases = []
        for x in (2 * pair, 2 * pair + 1):
            six = beside(v, 0, x) + [zup[x], zdn[x]]
            feats.append(jnp.concatenate([v[x]] + six, axis=0))
            bases.append(v[x] + viscosity * (sum(six[1:], six[0]) - 6.0 * v[x]))
        xin = jnp.concatenate(feats, axis=1).astype(BF)
        w = jnp.concatenate(
            [
                weight[8 * (x % 4) : 8 * (x % 4) + 8, 128 * (x // 4) : 128 * (x // 4) + 128]
                for x in (2 * pair, 2 * pair + 1)
            ],
            axis=1,
        )
        h1 = cat_y(jnp.tanh(dot(win_big, xin)).astype(BF))
        h2 = jnp.tanh(dot(wmid, h1)).astype(BF)
        h2s = stack_y(h2)
        corr = dot(wout_big, h2s) * w
        for i in range(2):
            new_ref[2 * pair + i] = bases[i] + corr[:, 128 * i : 128 * i + 128]
        dc = (jnp.concatenate([cot[2 * pair], cot[2 * pair + 1]], axis=1) * w).astype(BF)
        h2f = h2.astype(F32)
        h1f = h1.astype(F32)
        da2 = (cat_y(dot(wout_tbig, dc)) * (1.0 - h2f * h2f)).astype(BF)
        da1 = (dot(wmid_t, da2) * (1.0 - h1f * h1f)).astype(BF)
        da1s = stack_y(da1)
        df = dot(win_tbig, da1s)
        dfs += [df[:, :128], df[:, 128:]]
        gmid = gmid + dot_nt(da2, h1)
        gin = gin + dot_nt(xin, da1s)
        gout = gout + dot_nt(dc, h2s)

    both = jnp.concatenate([gin, gout], axis=0)
    both = jnp.where(iota((64, 512), 0) % 8 == iota((64, 512), 1) // 64, both, 0.0)
    both = jnp.sum(both.reshape(8, 8, 512), axis=1)
    both = both[:, 0:128] + both[:, 128:256] + both[:, 256:384] + both[:, 384:512]
    both = both + pltpu.roll(both, 64, 1)
    thin = jnp.concatenate([both[:, :64], jnp.zeros((56, 64), F32)], axis=0)
    parts[...] = jnp.concatenate([gmid, thin], axis=1).reshape(n, rows, 128)

    def send(src, dst, ssem, rsem, peer):
        copy = pltpu.make_async_remote_copy(
            src_ref=src, dst_ref=dst, send_sem=ssem, recv_sem=rsem, device_id=peer, device_id_type=MESH
        )
        return copy

    rs = []
    for d in range(1, n):
        peer = lax.rem(px + d, n)
        copy = send(parts.at[peer], rsbuf.at[d - 1], rs_ssem.at[d - 1], rs_rsem.at[d - 1], (peer, py))
        copy.start()
        rs.append(copy)

    ssend[0] = dfs[0][16:24]
    ssend[1] = dfs[7][8:16]
    for x in range(8):
        ssend[2, x : x + 1] = dfs[x][32:33]
        ssend[3, x : x + 1] = dfs[x][31:32]
    side = [
        pltpu.make_async_remote_copy(
            src_ref=ssend.at[k], dst_ref=srecv.at[k], send_sem=ss_sem.at[k], recv_sem=sr_sem.at[k],
            device_id=near[k], device_id_type=MESH,
        )
        for k in range(4)
    ]
    for copy in side:
        copy.start()

    for copy in rs:
        copy.wait()
    mine = parts[px]
    for d in range(n - 1):
        mine = mine + rsbuf[d]

    gybuf[py] = mine
    gy = []
    for d in range(1, m):
        peer = lax.rem(py + d, m)
        copy = send(gybuf.at[py], gybuf.at[py], gy_ssem.at[d - 1], gy_rsem.at[d - 1], (px, peer))
        copy.start()
        gy.append(copy)

    for copy in side:
        copy.wait()
    for x in range(8):
        six = beside(cot, 1, x) + [pltpu.roll(cot[x], 127, 1), pltpu.roll(cot[x], 1, 1)]
        out = cot[x] + viscosity * (sum(six[1:], six[0]) - 6.0 * cot[x])
        df = dfs[x]
        out = out + df[0:8] + pltpu.roll(df[40:48], 1, 1) + pltpu.roll(df[48:56], 127, 1)
        out = out + (dfs[x - 1][8:16] if x > 0 else srecv[1])
        out = out + (dfs[x + 1][16:24] if x < 7 else srecv[0])
        out = out + jnp.where(row == 0, srecv[3, x : x + 1, :], pltpu.roll(df[24:32], 1, 0))
        out = out + jnp.where(row == 7, srecv[2, x : x + 1, :], pltpu.roll(df[32:40], 7, 0))
        grad_ref[x] = out

    for copy in gy:
        copy.wait()
    total = gybuf[0]
    for d in range(1, m):
        total = total + gybuf[d]
    scale = 1.0 / jnp.sqrt(jnp.float32(n * m * ids_ref.shape[1] * 64))
    agbuf[px] = total * scale
    ag = []
    for d in range(1, n):
        copy = send(agbuf.at[px], agbuf.at[px], ag_ssem.at[d - 1], ag_rsem.at[d - 1], (lax.rem(px + d, n), py))
        copy.start()
        ag.append(copy)
    for copy in ag:
        copy.wait()
    tot_ref[...] = agbuf[...].reshape(n * rows, 128)


def body(n, m, velocity, cotangent, block_ids, fluid_count, fluid_cells, w_in, w_mid, w_out):
    slots = block_ids.shape[2]
    width = w_mid.shape[0]
    rows = -(-width // n)
    vmem = pl.BlockSpec(memory_space=pltpu.VMEM)
    dma = pltpu.SemaphoreType.DMA
    new_field, grad_field, total = pl.pallas_call(
        functools.partial(kernel, n, m),
        out_shape=(
            jax.ShapeDtypeStruct(velocity.shape, F32),
            jax.ShapeDtypeStruct(velocity.shape, F32),
            jax.ShapeDtypeStruct((n * rows, 128), F32),
        ),
        in_specs=[vmem] * 8,
        out_specs=(vmem, vmem, vmem),
        scratch_shapes=[
            pltpu.VMEM((4, 2, 8, 128), F32),
            pltpu.VMEM((4, 2, 8, 128), F32),
            pltpu.VMEM((4, 8, 128), F32),
            pltpu.VMEM((4, 8, 128), F32),
            pltpu.VMEM((n, rows, 128), F32),
            pltpu.VMEM((n - 1, rows, 128), F32),
            pltpu.VMEM((m, rows, 128), F32),
            pltpu.VMEM((n, rows, 128), F32),
            dma((4,)), dma((4,)), dma((4,)), dma((4,)),
            dma((n - 1,)), dma((n - 1,)), dma((m - 1,)), dma((m - 1,)), dma((n - 1,)), dma((n - 1,)),
        ],
        compiler_params=pltpu.CompilerParams(
            collective_id=0, has_side_effects=True, vmem_limit_bytes=48 * 1024 * 1024
        ),
    )(
        velocity,
        cotangent,
        block_ids.reshape(1, slots),
        fluid_count,
        fluid_cells.reshape(slots // 2, 128),
        w_in,
        w_mid,
        w_out,
    )
    return (
        new_field,
        grad_field,
        total[: w_in.shape[1], width : 2 * width].T,
        total[:width, :width],
        total[w_in.shape[1] : w_in.shape[1] + 1, width : 2 * width],
    )


def solution(mesh):
    n, m = mesh.shape["gx"], mesh.shape["gy"]
    in_specs = (
        P("gx", "gy", None),
        P("gx", "gy", None),
        P("gx", "gy", None),
        P("gx", "gy"),
        P("gx", "gy", None),
        P(),
        P(),
        P(),
    )
    out_specs = (P("gx", "gy", None), P("gx", "gy", None), P(), P(), P())
    return jax.shard_map(
        functools.partial(body, n, m), mesh=mesh, in_specs=in_specs, out_specs=out_specs, check_vma=False
    )
```

```python
import functools

import jax
import jax.numpy as jnp
from jax import lax
from jax.experimental import pallas as pl
from jax.experimental.pallas import tpu as pltpu
from jax.sharding import PartitionSpec as P

viscosity = 0.1
MESH = pl.DeviceIdType.MESH
BF = jnp.bfloat16
F32 = jnp.float32


def iota(shape, dim):
    return lax.broadcasted_iota(jnp.int32, shape, dim)


def dot(a, b):
    return jnp.dot(a, b, preferred_element_type=F32)


def dot_nt(a, b):
    return lax.dot_general(a, b, (((1,), (1,)), ((), ())), preferred_element_type=F32)


def ones_where(mask):
    return jnp.where(mask, 1.0, 0.0).astype(BF)


def fluid_field(ids, count, fluid2):
    half, lanes = fluid2.shape
    cells = lanes // 2
    slots = ids.shape[1]
    lane = iota((1, slots), 1)
    live = jnp.where(lane < count, ids, -1).astype(F32)
    spread = jnp.broadcast_to(live, (half, slots))
    slot_of = iota((half, slots), 1)
    row = iota((half, slots), 0)
    fluid_t = jnp.transpose(fluid2.astype(F32)).astype(BF)
    block = iota((half, 512), 1) // 4
    placed = None
    for h in range(2):
        col = jnp.sum(jnp.where(slot_of == 2 * row + h, spread, 0.0), axis=1, keepdims=True)
        hot = ones_where(jnp.broadcast_to(col, (half, 512)) == block.astype(F32))
        part = dot(fluid_t[h * cells : (h + 1) * cells], hot)
        placed = part if placed is None else placed + part
    keep = (iota((cells, 512), 0) % 4) == (iota((cells, 512), 1) % 4)
    placed = jnp.where(keep, placed, 0.0).astype(BF)
    rhs = jnp.concatenate(
        [
            jnp.concatenate([placed[:, 0:128], placed[:, 256:384]], axis=1),
            jnp.concatenate([placed[:, 128:256], placed[:, 384:512]], axis=1),
        ],
        axis=0,
    )
    r = iota((32, 2 * cells), 0)
    c = iota((32, 2 * cells), 1)
    pick = (r // 8 == (c % 64) // 16) & ((r % 8) // 4 == c // 64) & (r % 4 == (c % 16) // 4)
    return dot(ones_where(pick), rhs)


def kernel(
    n, m, v_hbm, c_hbm, ids_hbm, count_ref, fluid_hbm, win_hbm, wmid_hbm, wout_hbm,
    new_hbm, grad_hbm, gin_hbm, gmid_hbm, gout_hbm,
    new_ref, grad_ref, gin_ref, gmid_ref, gout_ref, out_sem,
    v_ref, c_ref, ids_ref, fluid_ref, win_ref, wmid_ref, wout_ref, in_sem,
    hsend, hrecv, ssend, srecv, parts, rsbuf, gybuf, agbuf,
    hs_sem, hr_sem, ss_sem, sr_sem, rs_ssem, rs_rsem, gy_ssem, gy_rsem, ag_ssem, ag_rsem,
):
    px = lax.axis_index("gx")
    py = lax.axis_index("gy")
    rows = parts.shape[1]

    loads = [
        pltpu.make_async_copy(src, dst, in_sem.at[k])
        for k, (src, dst) in enumerate(
            (
                (v_hbm, v_ref),
                (c_hbm, c_ref),
                (ids_hbm, ids_ref),
                (fluid_hbm, fluid_ref),
                (win_hbm, win_ref),
                (wmid_hbm, wmid_ref),
                (wout_hbm, wout_ref),
            )
        )
    ]
    for load in loads:
        load.start()

    barrier = pltpu.get_barrier_semaphore()
    for d in range(1, n):
        pl.semaphore_signal(barrier, inc=1, device_id=(lax.rem(px + d, n), py), device_id_type=MESH)
    for d in range(1, m):
        pl.semaphore_signal(barrier, inc=1, device_id=(px, lax.rem(py + d, m)), device_id_type=MESH)

    loads[0].wait()
    loads[1].wait()
    v = v_ref[...]
    cot = c_ref[...]
    for f, field in enumerate((v, cot)):
        hsend[0, f] = field[0]
        hsend[1, f] = field[7]
        hsend[2, f] = field[:, 0, :]
        hsend[3, f] = field[:, 7, :]
    near = (
        (lax.rem(px + n - 1, n), py),
        (lax.rem(px + 1, n), py),
        (px, lax.rem(py + m - 1, m)),
        (px, lax.rem(py + 1, m)),
    )
    pl.semaphore_wait(barrier, n + m - 2)
    halo = [
        pltpu.make_async_remote_copy(
            src_ref=hsend.at[k], dst_ref=hrecv.at[k], send_sem=hs_sem.at[k], recv_sem=hr_sem.at[k],
            device_id=near[k], device_id_type=MESH,
        )
        for k in range(4)
    ]
    for copy in halo:
        copy.start()

    for load in loads[2:]:
        load.wait()
    weight = fluid_field(ids_ref[...], count_ref[...], fluid_ref[...])
    win = win_ref[...]
    wmid = wmid_ref[...]
    wout = wout_ref[...]
    eye = ones_where(iota((64, 64), 0) == iota((64, 64), 1))
    wmid_t = dot_nt(eye, wmid).astype(BF)
    widen = ones_where(iota((7, 56), 0) == iota((7, 56), 1) // 8)
    win_y = dot(dot_nt(eye, win).astype(BF), widen)
    tall = jnp.concatenate([win_y] * 8, axis=0)
    win_big = jnp.where(iota((512, 56), 0) // 64 == iota((512, 56), 1) % 8, tall, 0.0).astype(BF)
    repeat = ones_where(iota((64, 512), 0) == iota((64, 512), 1) % 64)
    widen_t = ones_where(iota((56, 7), 1) == iota((56, 7), 0) // 8)
    win_t = dot(dot(widen_t, win).astype(BF), repeat)
    same_y = iota((56, 512), 0) % 8 == iota((56, 512), 1) // 64
    win_tbig = jnp.where(same_y, win_t, 0.0).astype(BF)
    wout_row = jnp.broadcast_to(dot(wout, repeat), (8, 512))
    wout_big = jnp.where(iota((8, 512), 0) == iota((8, 512), 1) // 64, wout_row, 0.0).astype(BF)
    wout_col = jnp.concatenate([dot_nt(eye, jnp.broadcast_to(wout, (8, 64)))] * 8, axis=0)
    wout_tbig = jnp.where(iota((512, 8), 0) // 64 == iota((512, 8), 1), wout_col, 0.0).astype(BF)

    row = iota((8, 128), 0)
    zup = [pltpu.roll(v[x], 127, 1) for x in range(8)]
    zdn = [pltpu.roll(v[x], 1, 1) for x in range(8)]

    for copy in halo:
        copy.wait()

    def beside(field, f, x):
        up = field[x + 1] if x < 7 else hrecv[0, f]
        down = field[x - 1] if x > 0 else hrecv[1, f]
        north = jnp.where(row == 7, hrecv[2, f, x : x + 1, :], pltpu.roll(field[x], 7, 0))
        south = jnp.where(row == 0, hrecv[3, f, x : x + 1, :], pltpu.roll(field[x], 1, 0))
        return [up, down, north, south]

    def cat_y(a):
        return jnp.concatenate([a[64 * y : 64 * y + 64] for y in range(8)], axis=1)

    def stack_y(a):
        return jnp.concatenate([a[:, 256 * y : 256 * y + 256] for y in range(8)], axis=0)

    gmid = jnp.zeros((64, 64), F32)
    gin = jnp.zeros((56, 512), F32)
    gout = jnp.zeros((8, 512), F32)
    dfs = []
    for pair in range(4):
        feats = []
        bases = []
        for x in (2 * pair, 2 * pair + 1):
            six = beside(v, 0, x) + [zup[x], zdn[x]]
            feats.append(jnp.concatenate([v[x]] + six, axis=0))
            bases.append(v[x] + viscosity * (sum(six[1:], six[0]) - 6.0 * v[x]))
        xin = jnp.concatenate(feats, axis=1).astype(BF)
        w = jnp.concatenate(
            [
                weight[8 * (x % 4) : 8 * (x % 4) + 8, 128 * (x // 4) : 128 * (x // 4) + 128]
                for x in (2 * pair, 2 * pair + 1)
            ],
            axis=1,
        )
        h1 = cat_y(jnp.tanh(dot(win_big, xin)).astype(BF))
        h2 = jnp.tanh(dot(wmid, h1)).astype(BF)
        h2s = stack_y(h2)
        corr = dot(wout_big, h2s) * w
        for i in range(2):
            new_ref[2 * pair + i] = bases[i] + corr[:, 128 * i : 128 * i + 128]
        dc = (jnp.concatenate([cot[2 * pair], cot[2 * pair + 1]], axis=1) * w).astype(BF)
        h2f = h2.astype(F32)
        h1f = h1.astype(F32)
        da2 = (cat_y(dot(wout_tbig, dc)) * (1.0 - h2f * h2f)).astype(BF)
        da1 = (dot(wmid_t, da2) * (1.0 - h1f * h1f)).astype(BF)
        da1s = stack_y(da1)
        df = dot(win_tbig, da1s)
        dfs += [df[:, :128], df[:, 128:]]
        gmid = gmid + dot_nt(da2, h1)
        gin = gin + dot_nt(xin, da1s)
        gout = gout + dot_nt(dc, h2s)

    both = jnp.concatenate([gin, gout], axis=0)
    both = jnp.where(iota((64, 512), 0) % 8 == iota((64, 512), 1) // 64, both, 0.0)
    both = jnp.sum(both.reshape(8, 8, 512), axis=1)
    both = both[:, 0:128] + both[:, 128:256] + both[:, 256:384] + both[:, 384:512]
    both = both + pltpu.roll(both, 64, 1)
    thin = jnp.concatenate([both[:, :64], jnp.zeros((56, 64), F32)], axis=0)
    parts[...] = jnp.concatenate([gmid, thin], axis=1).reshape(n, rows, 128)

    def send(src, dst, ssem, rsem, peer):
        copy = pltpu.make_async_remote_copy(
            src_ref=src, dst_ref=dst, send_sem=ssem, recv_sem=rsem, device_id=peer, device_id_type=MESH
        )
        return copy

    rs = []
    for d in range(1, n):
        peer = lax.rem(px + d, n)
        copy = send(parts.at[peer], rsbuf.at[d - 1], rs_ssem.at[d - 1], rs_rsem.at[d - 1], (peer, py))
        copy.start()
        rs.append(copy)

    ssend[0] = dfs[0][16:24]
    ssend[1] = dfs[7][8:16]
    for x in range(8):
        ssend[2, x : x + 1] = dfs[x][32:33]
        ssend[3, x : x + 1] = dfs[x][31:32]
    side = [
        pltpu.make_async_remote_copy(
            src_ref=ssend.at[k], dst_ref=srecv.at[k], send_sem=ss_sem.at[k], recv_sem=sr_sem.at[k],
            device_id=near[k], device_id_type=MESH,
        )
        for k in range(4)
    ]
    for copy in side:
        copy.start()

    for copy in rs:
        copy.wait()
    mine = parts[px]
    for d in range(n - 1):
        mine = mine + rsbuf[d]

    gybuf[py] = mine
    gy = []
    for d in range(1, m):
        peer = lax.rem(py + d, m)
        copy = send(gybuf.at[py], gybuf.at[py], gy_ssem.at[d - 1], gy_rsem.at[d - 1], (px, peer))
        copy.start()
        gy.append(copy)

    new_out = pltpu.make_async_copy(new_ref, new_hbm, out_sem.at[0])
    new_out.start()

    for copy in side:
        copy.wait()
    for x in range(8):
        six = beside(cot, 1, x) + [pltpu.roll(cot[x], 127, 1), pltpu.roll(cot[x], 1, 1)]
        out = cot[x] + viscosity * (sum(six[1:], six[0]) - 6.0 * cot[x])
        df = dfs[x]
        out = out + df[0:8] + pltpu.roll(df[40:48], 1, 1) + pltpu.roll(df[48:56], 127, 1)
        out = out + (dfs[x - 1][8:16] if x > 0 else srecv[1])
        out = out + (dfs[x + 1][16:24] if x < 7 else srecv[0])
        out = out + jnp.where(row == 0, srecv[3, x : x + 1, :], pltpu.roll(df[24:32], 1, 0))
        out = out + jnp.where(row == 7, srecv[2, x : x + 1, :], pltpu.roll(df[32:40], 7, 0))
        grad_ref[x] = out
    grad_out = pltpu.make_async_copy(grad_ref, grad_hbm, out_sem.at[1])
    grad_out.start()

    for copy in gy:
        copy.wait()
    total = gybuf[0]
    for d in range(1, m):
        total = total + gybuf[d]
    scale = 1.0 / jnp.sqrt(jnp.float32(n * m * ids_ref.shape[1] * 64))
    agbuf[px] = total * scale
    ag = []
    for d in range(1, n):
        copy = send(agbuf.at[px], agbuf.at[px], ag_ssem.at[d - 1], ag_rsem.at[d - 1], (lax.rem(px + d, n), py))
        copy.start()
        ag.append(copy)
    for copy in ag:
        copy.wait()
    total = agbuf[...].reshape(n * rows, 128)
    gmid_ref[...] = total[:64, :64]
    last = pltpu.roll(total[:8], 64, 1)[:, :64]
    gin_ref[...] = last[:7]
    gout_ref[...] = last[7:8]
    outs = [
        pltpu.make_async_copy(gin_ref, gin_hbm, out_sem.at[2]),
        pltpu.make_async_copy(gmid_ref, gmid_hbm, out_sem.at[3]),
        pltpu.make_async_copy(gout_ref, gout_hbm, out_sem.at[4]),
    ]
    for copy in outs:
        copy.start()
    for copy in [new_out, grad_out] + outs:
        copy.wait()


def hand_on(*refs):
    sem = refs[-1]
    half = len(refs) // 2
    copies = [pltpu.make_async_copy(refs[k], refs[half + k], sem.at[k]) for k in range(half)]
    for copy in copies:
        copy.start()
    for copy in copies:
        copy.wait()


def body(n, m, velocity, cotangent, block_ids, fluid_count, fluid_cells, w_in, w_mid, w_out):
    slots = block_ids.shape[2]
    width = w_mid.shape[0]
    rows = -(-width // n)
    vmem = pl.BlockSpec(memory_space=pltpu.VMEM)
    hbm = pl.BlockSpec(memory_space=pltpu.HBM)
    dma = pltpu.SemaphoreType.DMA
    outs = (
        jax.ShapeDtypeStruct(velocity.shape, F32),
        jax.ShapeDtypeStruct(velocity.shape, F32),
        jax.ShapeDtypeStruct(w_in.shape[::-1], F32),
        jax.ShapeDtypeStruct(w_mid.shape, F32),
        jax.ShapeDtypeStruct(w_out.shape, F32),
    )
    results = pl.pallas_call(
        functools.partial(kernel, n, m),
        out_shape=outs,
        in_specs=[hbm] * 3 + [vmem] + [hbm] * 4,
        out_specs=(hbm,) * 5,
        scratch_shapes=[pltpu.VMEM(out.shape, F32) for out in outs]
        + [
            dma((5,)),
            pltpu.VMEM(velocity.shape, F32),
            pltpu.VMEM(velocity.shape, F32),
            pltpu.VMEM((1, slots), jnp.int32),
            pltpu.VMEM((slots // 2, 128), jnp.int32),
            pltpu.VMEM(w_in.shape[::-1], BF),
            pltpu.VMEM(w_mid.shape, BF),
            pltpu.VMEM(w_out.shape, BF),
            dma((7,)),
            pltpu.VMEM((4, 2, 8, 128), F32),
            pltpu.VMEM((4, 2, 8, 128), F32),
            pltpu.VMEM((4, 8, 128), F32),
            pltpu.VMEM((4, 8, 128), F32),
            pltpu.VMEM((n, rows, 128), F32),
            pltpu.VMEM((n - 1, rows, 128), F32),
            pltpu.VMEM((m, rows, 128), F32),
            pltpu.VMEM((n, rows, 128), F32),
            dma((4,)), dma((4,)), dma((4,)), dma((4,)),
            dma((n - 1,)), dma((n - 1,)), dma((m - 1,)), dma((m - 1,)), dma((n - 1,)), dma((n - 1,)),
        ],
        compiler_params=pltpu.CompilerParams(
            collective_id=0, has_side_effects=True, vmem_limit_bytes=65300 * 1024
        ),
    )(
        velocity,
        cotangent,
        block_ids.reshape(1, slots),
        fluid_count,
        fluid_cells.reshape(slots // 2, 128),
        w_in.T,
        w_mid,
        w_out,
    )
    new_field, grad_field, gin_t, gmid, gout = pl.pallas_call(
        hand_on,
        out_shape=outs,
        in_specs=[hbm] * 5,
        out_specs=(hbm,) * 5,
        scratch_shapes=[dma((5,))],
        compiler_params=pltpu.CompilerParams(vmem_limit_bytes=65300 * 1024),
    )(*results)
    return new_field, grad_field, gin_t.T, gmid, gout


def solution(mesh):
    n, m = mesh.shape["gx"], mesh.shape["gy"]
    in_specs = (
        P("gx", "gy", None),
        P("gx", "gy", None),
        P("gx", "gy", None),
        P("gx", "gy"),
        P("gx", "gy", None),
        P(),
        P(),
        P(),
    )
    out_specs = (P("gx", "gy", None), P("gx", "gy", None), P(), P(), P())
    return jax.shard_map(
        functools.partial(body, n, m), mesh=mesh, in_specs=in_specs, out_specs=out_specs, check_vma=False
    )
```

```python
import functools

import jax
import jax.numpy as jnp
from jax import lax
from jax.experimental import pallas as pl
from jax.experimental.pallas import tpu as pltpu
from jax.sharding import PartitionSpec as P

viscosity = 0.1
MESH = pl.DeviceIdType.MESH
BF = jnp.bfloat16
F32 = jnp.float32


def iota(shape, dim):
    return lax.broadcasted_iota(jnp.int32, shape, dim)


def dot(a, b):
    return jnp.dot(a, b, preferred_element_type=F32)


def dot_nt(a, b):
    return lax.dot_general(a, b, (((1,), (1,)), ((), ())), preferred_element_type=F32)


def ones_where(mask):
    return jnp.where(mask, 1.0, 0.0).astype(BF)


def fluid_field(ids, count, fluid2):
    half, lanes = fluid2.shape
    cells = lanes // 2
    slots = ids.shape[1]
    lane = iota((1, slots), 1)
    live = jnp.where(lane < count, ids, -1).astype(F32)
    spread = jnp.broadcast_to(live, (half, slots))
    slot_of = iota((half, slots), 1)
    row = iota((half, slots), 0)
    fluid_t = jnp.transpose(fluid2.astype(F32)).astype(BF)
    block = iota((half, 512), 1) // 4
    placed = None
    for h in range(2):
        col = jnp.sum(jnp.where(slot_of == 2 * row + h, spread, 0.0), axis=1, keepdims=True)
        hot = ones_where(jnp.broadcast_to(col, (half, 512)) == block.astype(F32))
        part = dot(fluid_t[h * cells : (h + 1) * cells], hot)
        placed = part if placed is None else placed + part
    keep = (iota((cells, 512), 0) % 4) == (iota((cells, 512), 1) % 4)
    placed = jnp.where(keep, placed, 0.0).astype(BF)
    rhs = jnp.concatenate(
        [
            jnp.concatenate([placed[:, 0:128], placed[:, 256:384]], axis=1),
            jnp.concatenate([placed[:, 128:256], placed[:, 384:512]], axis=1),
        ],
        axis=0,
    )
    r = iota((32, 2 * cells), 0)
    c = iota((32, 2 * cells), 1)
    pick = (r // 8 == (c % 64) // 16) & ((r % 8) // 4 == c // 64) & (r % 4 == (c % 16) // 4)
    return dot(ones_where(pick), rhs)


def kernel(
    n, m, v_hbm, c_hbm, ids_hbm, count_ref, fluid_hbm, win_hbm, wmid_hbm, wout_hbm,
    new_hbm, grad_hbm, gin_hbm, gmid_hbm, gout_hbm,
    new_ref, grad_ref, gin_ref, gmid_ref, gout_ref, out_sem,
    v_ref, c_ref, ids_ref, fluid_ref, win_ref, wmid_ref, wout_ref, in_sem,
    hsend, hrecv, ssend, srecv, gybuf, agbuf,
    hs_sem, hr_sem, ss_sem, sr_sem, gy_ssem, gy_rsem, ag_ssem, ag_rsem,
):
    px = lax.axis_index("gx")
    py = lax.axis_index("gy")

    loads = [
        pltpu.make_async_copy(src, dst, in_sem.at[k])
        for k, (src, dst) in enumerate(
            (
                (v_hbm, v_ref),
                (c_hbm, c_ref),
                (ids_hbm, ids_ref),
                (fluid_hbm, fluid_ref),
                (win_hbm, win_ref),
                (wmid_hbm, wmid_ref),
                (wout_hbm, wout_ref),
            )
        )
    ]
    for load in loads:
        load.start()

    barrier = pltpu.get_barrier_semaphore()
    for d in range(1, n):
        pl.semaphore_signal(barrier, inc=1, device_id=(lax.rem(px + d, n), py), device_id_type=MESH)
    for d in range(1, m):
        pl.semaphore_signal(barrier, inc=1, device_id=(px, lax.rem(py + d, m)), device_id_type=MESH)

    loads[0].wait()
    loads[1].wait()
    v = v_ref[...]
    cot = c_ref[...]
    for f, field in enumerate((v, cot)):
        hsend[0, f] = field[0]
        hsend[1, f] = field[7]
        hsend[2, f] = field[:, 0, :]
        hsend[3, f] = field[:, 7, :]
    near = (
        (lax.rem(px + n - 1, n), py),
        (lax.rem(px + 1, n), py),
        (px, lax.rem(py + m - 1, m)),
        (px, lax.rem(py + 1, m)),
    )
    pl.semaphore_wait(barrier, n + m - 2)
    halo = [
        pltpu.make_async_remote_copy(
            src_ref=hsend.at[k, f], dst_ref=hrecv.at[k, f], send_sem=hs_sem.at[k, f], recv_sem=hr_sem.at[k, f],
            device_id=near[k], device_id_type=MESH,
        )
        for f in range(2)
        for k in (3, 2, 1, 0)
    ]
    for copy in halo:
        copy.start()

    for load in loads[2:]:
        load.wait()
    weight = fluid_field(ids_ref[...], count_ref[...], fluid_ref[...])
    win = win_ref[...]
    wmid = wmid_ref[...]
    wout = wout_ref[...]
    eye = ones_where(iota((64, 64), 0) == iota((64, 64), 1))
    wmid_t = dot_nt(eye, wmid).astype(BF)
    widen = ones_where(iota((7, 56), 0) == iota((7, 56), 1) // 8)
    win_y = dot(dot_nt(eye, win).astype(BF), widen)
    tall = jnp.concatenate([win_y] * 8, axis=0)
    win_big = jnp.where(iota((512, 56), 0) // 64 == iota((512, 56), 1) % 8, tall, 0.0).astype(BF)
    repeat = ones_where(iota((64, 512), 0) == iota((64, 512), 1) % 64)
    widen_t = ones_where(iota((56, 7), 1) == iota((56, 7), 0) // 8)
    win_t = dot(dot(widen_t, win).astype(BF), repeat)
    same_y = iota((56, 512), 0) % 8 == iota((56, 512), 1) // 64
    win_tbig = jnp.where(same_y, win_t, 0.0).astype(BF)
    wout_row = jnp.broadcast_to(dot(wout, repeat), (8, 512))
    wout_big = jnp.where(iota((8, 512), 0) == iota((8, 512), 1) // 64, wout_row, 0.0).astype(BF)
    wout_col = jnp.concatenate([dot_nt(eye, jnp.broadcast_to(wout, (8, 64)))] * 8, axis=0)
    wout_tbig = jnp.where(iota((512, 8), 0) // 64 == iota((512, 8), 1), wout_col, 0.0).astype(BF)

    row = iota((8, 128), 0)
    zup = [pltpu.roll(v[x], 127, 1) for x in range(8)]
    zdn = [pltpu.roll(v[x], 1, 1) for x in range(8)]

    for copy in halo[:4]:
        copy.wait()

    def beside(field, f, x):
        up = field[x + 1] if x < 7 else hrecv[0, f]
        down = field[x - 1] if x > 0 else hrecv[1, f]
        north = jnp.where(row == 7, hrecv[2, f, x : x + 1, :], pltpu.roll(field[x], 7, 0))
        south = jnp.where(row == 0, hrecv[3, f, x : x + 1, :], pltpu.roll(field[x], 1, 0))
        return [up, down, north, south]

    def cat_y(a):
        return jnp.concatenate([a[64 * y : 64 * y + 64] for y in range(8)], axis=1)

    def stack_y(a):
        return jnp.concatenate([a[:, 256 * y : 256 * y + 256] for y in range(8)], axis=0)

    gmid = jnp.zeros((64, 64), F32)
    gin = jnp.zeros((56, 512), F32)
    gout = jnp.zeros((8, 512), F32)
    dfs = []
    for pair in range(4):
        feats = []
        bases = []
        for x in (2 * pair, 2 * pair + 1):
            six = beside(v, 0, x) + [zup[x], zdn[x]]
            feats.append(jnp.concatenate([v[x]] + six, axis=0))
            bases.append(v[x] + viscosity * (sum(six[1:], six[0]) - 6.0 * v[x]))
        xin = jnp.concatenate(feats, axis=1).astype(BF)
        w = jnp.concatenate(
            [
                weight[8 * (x % 4) : 8 * (x % 4) + 8, 128 * (x // 4) : 128 * (x // 4) + 128]
                for x in (2 * pair, 2 * pair + 1)
            ],
            axis=1,
        )
        h1 = cat_y(jnp.tanh(dot(win_big, xin)).astype(BF))
        h2 = jnp.tanh(dot(wmid, h1)).astype(BF)
        h2s = stack_y(h2)
        corr = dot(wout_big, h2s) * w
        for i in range(2):
            new_ref[2 * pair + i] = bases[i] + corr[:, 128 * i : 128 * i + 128]
        dc = (jnp.concatenate([cot[2 * pair], cot[2 * pair + 1]], axis=1) * w).astype(BF)
        h2f = h2.astype(F32)
        h1f = h1.astype(F32)
        da2 = (cat_y(dot(wout_tbig, dc)) * (1.0 - h2f * h2f)).astype(BF)
        da1 = (dot(wmid_t, da2) * (1.0 - h1f * h1f)).astype(BF)
        da1s = stack_y(da1)
        df = dot(win_tbig, da1s)
        dfs += [df[:, :128], df[:, 128:]]
        gmid = gmid + dot_nt(da2, h1)
        gin = gin + dot_nt(xin, da1s)
        gout = gout + dot_nt(dc, h2s)

    both = jnp.concatenate([gin, gout], axis=0)
    both = jnp.where(iota((64, 512), 0) % 8 == iota((64, 512), 1) // 64, both, 0.0)
    both = jnp.sum(both.reshape(8, 8, 512), axis=1)
    both = both[:, 0:128] + both[:, 128:256] + both[:, 256:384] + both[:, 384:512]
    both = both + pltpu.roll(both, 64, 1)
    packed = jnp.concatenate([jnp.concatenate([gmid[:32], gmid[32:]], axis=1), both[:, :128]], axis=0)
    gybuf[py] = packed

    def send(src, dst, ssem, rsem, peer):
        copy = pltpu.make_async_remote_copy(
            src_ref=src, dst_ref=dst, send_sem=ssem, recv_sem=rsem, device_id=peer, device_id_type=MESH
        )
        return copy

    gy = []
    for d in range(1, m):
        peer = lax.rem(py + d, m)
        copy = send(gybuf.at[py], gybuf.at[py], gy_ssem.at[d - 1], gy_rsem.at[d - 1], (px, peer))
        copy.start()
        gy.append(copy)

    ssend[0] = dfs[0][16:24]
    ssend[1] = dfs[7][8:16]
    for x in range(8):
        ssend[2, x : x + 1] = dfs[x][32:33]
        ssend[3, x : x + 1] = dfs[x][31:32]
    side = [
        pltpu.make_async_remote_copy(
            src_ref=ssend.at[k], dst_ref=srecv.at[k], send_sem=ss_sem.at[k], recv_sem=sr_sem.at[k],
            device_id=near[k], device_id_type=MESH,
        )
        for k in range(4)
    ]
    for copy in side:
        copy.start()

    for copy in gy:
        copy.wait()
    total = gybuf[0]
    for d in range(1, m):
        total = total + gybuf[d]
    agbuf[px] = total
    ag = []
    for d in range(1, n):
        copy = send(agbuf.at[px], agbuf.at[px], ag_ssem.at[d - 1], ag_rsem.at[d - 1], (lax.rem(px + d, n), py))
        copy.start()
        ag.append(copy)

    new_out = pltpu.make_async_copy(new_ref, new_hbm, out_sem.at[0])
    new_out.start()

    for copy in halo[4:] + side:
        copy.wait()
    for x in range(8):
        six = beside(cot, 1, x) + [pltpu.roll(cot[x], 127, 1), pltpu.roll(cot[x], 1, 1)]
        out = cot[x] + viscosity * (sum(six[1:], six[0]) - 6.0 * cot[x])
        df = dfs[x]
        out = out + df[0:8] + pltpu.roll(df[40:48], 1, 1) + pltpu.roll(df[48:56], 127, 1)
        out = out + (dfs[x - 1][8:16] if x > 0 else srecv[1])
        out = out + (dfs[x + 1][16:24] if x < 7 else srecv[0])
        out = out + jnp.where(row == 0, srecv[3, x : x + 1, :], pltpu.roll(df[24:32], 1, 0))
        out = out + jnp.where(row == 7, srecv[2, x : x + 1, :], pltpu.roll(df[32:40], 7, 0))
        grad_ref[x] = out
    grad_out = pltpu.make_async_copy(grad_ref, grad_hbm, out_sem.at[1])
    grad_out.start()

    for copy in ag:
        copy.wait()
    total = agbuf[0]
    for d in range(1, n):
        total = total + agbuf[d]
    total = total * (1.0 / jnp.sqrt(jnp.float32(n * m * ids_ref.shape[1] * 64)))
    gmid_ref[...] = jnp.concatenate([total[:32, :64], pltpu.roll(total[:32], 64, 1)[:, :64]], axis=0)
    last = total[32:40, :64]
    gin_ref[...] = last[:7]
    gout_ref[...] = last[7:8]
    outs = [
        pltpu.make_async_copy(gin_ref, gin_hbm, out_sem.at[2]),
        pltpu.make_async_copy(gmid_ref, gmid_hbm, out_sem.at[3]),
        pltpu.make_async_copy(gout_ref, gout_hbm, out_sem.at[4]),
    ]
    for copy in outs:
        copy.start()
    for copy in [new_out, grad_out] + outs:
        copy.wait()


def hand_on(*refs):
    ins, outs, bufs, isem, osem = refs[:5], refs[5:10], refs[10:15], refs[15], refs[16]
    a = [pltpu.make_async_copy(ins[k], bufs[k], isem.at[k]) for k in range(5)]
    b = [pltpu.make_async_copy(bufs[k], outs[k], osem.at[k]) for k in range(5)]
    for copy in a:
        copy.start()
    for k in range(5):
        a[k].wait()
        b[k].start()
    for copy in b:
        copy.wait()


def body(n, m, velocity, cotangent, block_ids, fluid_count, fluid_cells, w_in, w_mid, w_out):
    slots = block_ids.shape[2]
    width = w_mid.shape[0]
    vmem = pl.BlockSpec(memory_space=pltpu.VMEM)
    hbm = pl.BlockSpec(memory_space=pltpu.HBM)
    dma = pltpu.SemaphoreType.DMA
    outs = (
        jax.ShapeDtypeStruct(velocity.shape, F32),
        jax.ShapeDtypeStruct(velocity.shape, F32),
        jax.ShapeDtypeStruct(w_in.shape[::-1], F32),
        jax.ShapeDtypeStruct(w_mid.shape, F32),
        jax.ShapeDtypeStruct(w_out.shape, F32),
    )
    results = pl.pallas_call(
        functools.partial(kernel, n, m),
        out_shape=outs,
        in_specs=[hbm] * 3 + [vmem] + [hbm] * 4,
        out_specs=(hbm,) * 5,
        scratch_shapes=[pltpu.VMEM(out.shape, F32) for out in outs]
        + [
            dma((5,)),
            pltpu.VMEM(velocity.shape, F32),
            pltpu.VMEM(velocity.shape, F32),
            pltpu.VMEM((1, slots), jnp.int32),
            pltpu.VMEM((slots // 2, 128), jnp.int32),
            pltpu.VMEM(w_in.shape[::-1], BF),
            pltpu.VMEM(w_mid.shape, BF),
            pltpu.VMEM(w_out.shape, BF),
            dma((7,)),
            pltpu.VMEM((4, 2, 8, 128), F32),
            pltpu.VMEM((4, 2, 8, 128), F32),
            pltpu.VMEM((4, 8, 128), F32),
            pltpu.VMEM((4, 8, 128), F32),
            pltpu.VMEM((m, width // 2 + 8, 128), F32),
            pltpu.VMEM((n, width // 2 + 8, 128), F32),
            dma((4, 2)), dma((4, 2)), dma((4,)), dma((4,)),
            dma((m - 1,)), dma((m - 1,)), dma((n - 1,)), dma((n - 1,)),
        ],
        compiler_params=pltpu.CompilerParams(
            collective_id=0, has_side_effects=True, vmem_limit_bytes=65300 * 1024
        ),
    )(
        velocity,
        cotangent,
        block_ids.reshape(1, slots),
        fluid_count,
        fluid_cells.reshape(slots // 2, 128),
        w_in.T,
        w_mid,
        w_out,
    )
    new_field, grad_field, gin_t, gmid, gout = pl.pallas_call(
        hand_on,
        out_shape=outs,
        in_specs=[hbm] * 5,
        out_specs=(hbm,) * 5,
        scratch_shapes=[pltpu.VMEM(out.shape, F32) for out in outs] + [dma((5,)), dma((5,))],
        compiler_params=pltpu.CompilerParams(vmem_limit_bytes=65300 * 1024),
    )(*results)
    return new_field, grad_field, gin_t.T, gmid, gout


def solution(mesh):
    n, m = mesh.shape["gx"], mesh.shape["gy"]
    in_specs = (
        P("gx", "gy", None),
        P("gx", "gy", None),
        P("gx", "gy", None),
        P("gx", "gy"),
        P("gx", "gy", None),
        P(),
        P(),
        P(),
    )
    out_specs = (P("gx", "gy", None), P("gx", "gy", None), P(), P(), P())
    return jax.shard_map(
        functools.partial(body, n, m), mesh=mesh, in_specs=in_specs, out_specs=out_specs, check_vma=False
    )
```

```python
import functools

import jax
import jax.numpy as jnp
from jax import lax
from jax.experimental import pallas as pl
from jax.experimental.pallas import tpu as pltpu
from jax.sharding import PartitionSpec as P

viscosity = 0.1
MESH = pl.DeviceIdType.MESH
BF = jnp.bfloat16
F32 = jnp.float32


def iota(shape, dim):
    return lax.broadcasted_iota(jnp.int32, shape, dim)


def dot(a, b):
    return jnp.dot(a, b, preferred_element_type=F32)


def dot_nt(a, b):
    return lax.dot_general(a, b, (((1,), (1,)), ((), ())), preferred_element_type=F32)


def ones_where(mask):
    return jnp.where(mask, 1.0, 0.0).astype(BF)


def fluid_field(ids, count, fluid2):
    half, lanes = fluid2.shape
    cells = lanes // 2
    slots = ids.shape[1]
    lane = iota((1, slots), 1)
    live = jnp.where(lane < count, ids, -1).astype(F32)
    spread = jnp.broadcast_to(live, (half, slots))
    slot_of = iota((half, slots), 1)
    row = iota((half, slots), 0)
    fluid_t = jnp.transpose(fluid2.astype(F32)).astype(BF)
    block = iota((half, 512), 1) // 4
    placed = None
    for h in range(2):
        col = jnp.sum(jnp.where(slot_of == 2 * row + h, spread, 0.0), axis=1, keepdims=True)
        hot = ones_where(jnp.broadcast_to(col, (half, 512)) == block.astype(F32))
        part = dot(fluid_t[h * cells : (h + 1) * cells], hot)
        placed = part if placed is None else placed + part
    keep = (iota((cells, 512), 0) % 4) == (iota((cells, 512), 1) % 4)
    placed = jnp.where(keep, placed, 0.0).astype(BF)
    rhs = jnp.concatenate(
        [
            jnp.concatenate([placed[:, 0:128], placed[:, 256:384]], axis=1),
            jnp.concatenate([placed[:, 128:256], placed[:, 384:512]], axis=1),
        ],
        axis=0,
    )
    r = iota((32, 2 * cells), 0)
    c = iota((32, 2 * cells), 1)
    pick = (r // 8 == (c % 64) // 16) & ((r % 8) // 4 == c // 64) & (r % 4 == (c % 16) // 4)
    return dot(ones_where(pick), rhs)


def kernel(
    n, m, v_hbm, c_hbm, ids_hbm, count_ref, fluid_hbm, win_hbm, wmid_hbm, wout_hbm,
    new_hbm, grad_hbm, gin_hbm, gmid_hbm, gout_hbm,
    new_ref, grad_ref, gin_ref, gmid_ref, gout_ref, out_sem,
    v_ref, c_ref, ids_ref, fluid_ref, win_ref, wmid_ref, wout_ref, in_sem,
    hsend, hrecv, ssend, srecv, gybuf, agbuf,
    hs_sem, hr_sem, ss_sem, sr_sem, gy_ssem, gy_rsem, ag_ssem, ag_rsem,
):
    px = lax.axis_index("gx")
    py = lax.axis_index("gy")

    loads = [
        pltpu.make_async_copy(src, dst, in_sem.at[k])
        for k, (src, dst) in enumerate(
            (
                (v_hbm, v_ref),
                (c_hbm, c_ref),
                (ids_hbm, ids_ref),
                (fluid_hbm, fluid_ref),
                (win_hbm, win_ref),
                (wmid_hbm, wmid_ref),
                (wout_hbm, wout_ref),
            )
        )
    ]
    for load in loads:
        load.start()

    barrier = pltpu.get_barrier_semaphore()
    for d in range(1, n):
        pl.semaphore_signal(barrier, inc=1, device_id=(lax.rem(px + d, n), py), device_id_type=MESH)
    for d in range(1, m):
        pl.semaphore_signal(barrier, inc=1, device_id=(px, lax.rem(py + d, m)), device_id_type=MESH)

    loads[0].wait()
    loads[1].wait()
    v = v_ref[...]
    cot = c_ref[...]
    for f, field in enumerate((v, cot)):
        hsend[0, f] = field[0]
        hsend[1, f] = field[7]
        hsend[2, f] = field[:, 0, :]
        hsend[3, f] = field[:, 7, :]
    near = (
        (lax.rem(px + n - 1, n), py),
        (lax.rem(px + 1, n), py),
        (px, lax.rem(py + m - 1, m)),
        (px, lax.rem(py + 1, m)),
    )
    pl.semaphore_wait(barrier, n + m - 2)
    halo = [
        pltpu.make_async_remote_copy(
            src_ref=hsend.at[k, f], dst_ref=hrecv.at[k, f], send_sem=hs_sem.at[k, f], recv_sem=hr_sem.at[k, f],
            device_id=near[k], device_id_type=MESH,
        )
        for f in range(2)
        for k in (3, 2, 1, 0)
    ]
    for copy in halo:
        copy.start()

    for load in loads[2:]:
        load.wait()
    weight = fluid_field(ids_ref[...], count_ref[...], fluid_ref[...])
    win = win_ref[...]
    wmid = wmid_ref[...]
    wout = wout_ref[...]
    eye = ones_where(iota((64, 64), 0) == iota((64, 64), 1))
    wmid_t = dot_nt(eye, wmid).astype(BF)
    widen = ones_where(iota((7, 56), 0) == iota((7, 56), 1) // 8)
    win_y = dot(dot_nt(eye, win).astype(BF), widen)
    tall = jnp.concatenate([win_y] * 8, axis=0)
    win_big = jnp.where(iota((512, 56), 0) // 64 == iota((512, 56), 1) % 8, tall, 0.0).astype(BF)
    repeat = ones_where(iota((64, 512), 0) == iota((64, 512), 1) % 64)
    widen_t = ones_where(iota((56, 7), 1) == iota((56, 7), 0) // 8)
    win_t = dot(dot(widen_t, win).astype(BF), repeat)
    same_y = iota((56, 512), 0) % 8 == iota((56, 512), 1) // 64
    win_tbig = jnp.where(same_y, win_t, 0.0).astype(BF)
    wout_row = jnp.broadcast_to(dot(wout, repeat), (8, 512))
    wout_big = jnp.where(iota((8, 512), 0) == iota((8, 512), 1) // 64, wout_row, 0.0).astype(BF)
    wout_col = jnp.concatenate([dot_nt(eye, jnp.broadcast_to(wout, (8, 64)))] * 8, axis=0)
    wout_tbig = jnp.where(iota((512, 8), 0) // 64 == iota((512, 8), 1), wout_col, 0.0).astype(BF)

    row = iota((8, 128), 0)
    zup = [pltpu.roll(v[x], 127, 1) for x in range(8)]
    zdn = [pltpu.roll(v[x], 1, 1) for x in range(8)]

    for copy in halo[:4]:
        copy.wait()

    def beside(field, f, x):
        up = field[x + 1] if x < 7 else hrecv[0, f]
        down = field[x - 1] if x > 0 else hrecv[1, f]
        north = jnp.where(row == 7, hrecv[2, f, x : x + 1, :], pltpu.roll(field[x], 7, 0))
        south = jnp.where(row == 0, hrecv[3, f, x : x + 1, :], pltpu.roll(field[x], 1, 0))
        return [up, down, north, south]

    def cat_y(a):
        return jnp.concatenate([a[64 * y : 64 * y + 64] for y in range(8)], axis=1)

    def stack_y(a):
        return jnp.concatenate([a[:, 256 * y : 256 * y + 256] for y in range(8)], axis=0)

    gmid = jnp.zeros((64, 64), F32)
    gin = jnp.zeros((56, 512), F32)
    gout = jnp.zeros((8, 512), F32)
    later = []
    for pair in range(4):
        feats = []
        bases = []
        for x in (2 * pair, 2 * pair + 1):
            six = beside(v, 0, x) + [zup[x], zdn[x]]
            feats.append(jnp.concatenate([v[x]] + six, axis=0))
            bases.append(v[x] + viscosity * (sum(six[1:], six[0]) - 6.0 * v[x]))
        xin = jnp.concatenate(feats, axis=1).astype(BF)
        w = jnp.concatenate(
            [
                weight[8 * (x % 4) : 8 * (x % 4) + 8, 128 * (x // 4) : 128 * (x // 4) + 128]
                for x in (2 * pair, 2 * pair + 1)
            ],
            axis=1,
        )
        h1 = cat_y(jnp.tanh(dot(win_big, xin)).astype(BF))
        h2 = jnp.tanh(dot(wmid, h1)).astype(BF)
        h2s = stack_y(h2)
        dc = (jnp.concatenate([cot[2 * pair], cot[2 * pair + 1]], axis=1) * w).astype(BF)
        h2f = h2.astype(F32)
        h1f = h1.astype(F32)
        da2 = (cat_y(dot(wout_tbig, dc)) * (1.0 - h2f * h2f)).astype(BF)
        da1 = (dot(wmid_t, da2) * (1.0 - h1f * h1f)).astype(BF)
        da1s = stack_y(da1)
        later.append((bases, h2s, w, da1s))
        gmid = gmid + dot_nt(da2, h1)
        gin = gin + dot_nt(xin, da1s)
        gout = gout + dot_nt(dc, h2s)

    both = jnp.concatenate([gin, gout], axis=0)
    both = jnp.where(iota((64, 512), 0) % 8 == iota((64, 512), 1) // 64, both, 0.0)
    both = jnp.sum(both.reshape(8, 8, 512), axis=1)
    both = both[:, 0:128] + both[:, 128:256] + both[:, 256:384] + both[:, 384:512]
    both = both + pltpu.roll(both, 64, 1)
    packed = jnp.concatenate([jnp.concatenate([gmid[:32], gmid[32:]], axis=1), both[:, :128]], axis=0)
    gybuf[py] = packed

    def send(src, dst, ssem, rsem, peer):
        copy = pltpu.make_async_remote_copy(
            src_ref=src, dst_ref=dst, send_sem=ssem, recv_sem=rsem, device_id=peer, device_id_type=MESH
        )
        return copy

    gy = []
    for d in range(1, m):
        peer = lax.rem(py + d, m)
        copy = send(gybuf.at[py], gybuf.at[py], gy_ssem.at[d - 1], gy_rsem.at[d - 1], (px, peer))
        copy.start()
        gy.append(copy)

    dfs = []
    for _, _, _, da1s in later:
        df = dot(win_tbig, da1s)
        dfs += [df[:, :128], df[:, 128:]]
    ssend[0] = dfs[0][16:24]
    ssend[1] = dfs[7][8:16]
    for x in range(8):
        ssend[2, x : x + 1] = dfs[x][32:33]
        ssend[3, x : x + 1] = dfs[x][31:32]
    side = [
        pltpu.make_async_remote_copy(
            src_ref=ssend.at[k], dst_ref=srecv.at[k], send_sem=ss_sem.at[k], recv_sem=sr_sem.at[k],
            device_id=near[k], device_id_type=MESH,
        )
        for k in range(4)
    ]
    for copy in side:
        copy.start()

    for pair, (bases, h2s, w, _) in enumerate(later):
        corr = dot(wout_big, h2s) * w
        for i in range(2):
            new_ref[2 * pair + i] = bases[i] + corr[:, 128 * i : 128 * i + 128]

    for copy in gy:
        copy.wait()
    total = gybuf[0]
    for d in range(1, m):
        total = total + gybuf[d]
    agbuf[px] = total
    ag = []
    for d in range(1, n):
        copy = send(agbuf.at[px], agbuf.at[px], ag_ssem.at[d - 1], ag_rsem.at[d - 1], (lax.rem(px + d, n), py))
        copy.start()
        ag.append(copy)

    new_out = pltpu.make_async_copy(new_ref, new_hbm, out_sem.at[0])
    new_out.start()

    for copy in halo[4:] + side:
        copy.wait()
    for x in range(8):
        six = beside(cot, 1, x) + [pltpu.roll(cot[x], 127, 1), pltpu.roll(cot[x], 1, 1)]
        out = cot[x] + viscosity * (sum(six[1:], six[0]) - 6.0 * cot[x])
        df = dfs[x]
        out = out + df[0:8] + pltpu.roll(df[40:48], 1, 1) + pltpu.roll(df[48:56], 127, 1)
        out = out + (dfs[x - 1][8:16] if x > 0 else srecv[1])
        out = out + (dfs[x + 1][16:24] if x < 7 else srecv[0])
        out = out + jnp.where(row == 0, srecv[3, x : x + 1, :], pltpu.roll(df[24:32], 1, 0))
        out = out + jnp.where(row == 7, srecv[2, x : x + 1, :], pltpu.roll(df[32:40], 7, 0))
        grad_ref[x] = out
    grad_out = pltpu.make_async_copy(grad_ref, grad_hbm, out_sem.at[1])
    grad_out.start()

    for copy in ag:
        copy.wait()
    total = agbuf[0]
    for d in range(1, n):
        total = total + agbuf[d]
    total = total * (1.0 / jnp.sqrt(jnp.float32(n * m * ids_ref.shape[1] * 64)))
    gmid_ref[...] = jnp.concatenate([total[:32, :64], pltpu.roll(total[:32], 64, 1)[:, :64]], axis=0)
    last = total[32:40, :64]
    gin_ref[...] = last[:7]
    gout_ref[...] = last[7:8]
    outs = [
        pltpu.make_async_copy(gin_ref, gin_hbm, out_sem.at[2]),
        pltpu.make_async_copy(gmid_ref, gmid_hbm, out_sem.at[3]),
        pltpu.make_async_copy(gout_ref, gout_hbm, out_sem.at[4]),
    ]
    for copy in outs:
        copy.start()
    for copy in [new_out, grad_out] + outs:
        copy.wait()


def hand_on(*refs):
    ins, outs, bufs, isem, osem = refs[:5], refs[5:10], refs[10:15], refs[15], refs[16]
    a = [pltpu.make_async_copy(ins[k], bufs[k], isem.at[k]) for k in range(5)]
    b = [pltpu.make_async_copy(bufs[k], outs[k], osem.at[k]) for k in range(5)]
    for copy in a:
        copy.start()
    for k in range(5):
        a[k].wait()
        b[k].start()
    for copy in b:
        copy.wait()


def body(n, m, velocity, cotangent, block_ids, fluid_count, fluid_cells, w_in, w_mid, w_out):
    slots = block_ids.shape[2]
    width = w_mid.shape[0]
    vmem = pl.BlockSpec(memory_space=pltpu.VMEM)
    hbm = pl.BlockSpec(memory_space=pltpu.HBM)
    dma = pltpu.SemaphoreType.DMA
    outs = (
        jax.ShapeDtypeStruct(velocity.shape, F32),
        jax.ShapeDtypeStruct(velocity.shape, F32),
        jax.ShapeDtypeStruct(w_in.shape[::-1], F32),
        jax.ShapeDtypeStruct(w_mid.shape, F32),
        jax.ShapeDtypeStruct(w_out.shape, F32),
    )
    results = pl.pallas_call(
        functools.partial(kernel, n, m),
        out_shape=outs,
        in_specs=[hbm] * 3 + [vmem] + [hbm] * 4,
        out_specs=(hbm,) * 5,
        scratch_shapes=[pltpu.VMEM(out.shape, F32) for out in outs]
        + [
            dma((5,)),
            pltpu.VMEM(velocity.shape, F32),
            pltpu.VMEM(velocity.shape, F32),
            pltpu.VMEM((1, slots), jnp.int32),
            pltpu.VMEM((slots // 2, 128), jnp.int32),
            pltpu.VMEM(w_in.shape[::-1], BF),
            pltpu.VMEM(w_mid.shape, BF),
            pltpu.VMEM(w_out.shape, BF),
            dma((7,)),
            pltpu.VMEM((4, 2, 8, 128), F32),
            pltpu.VMEM((4, 2, 8, 128), F32),
            pltpu.VMEM((4, 8, 128), F32),
            pltpu.VMEM((4, 8, 128), F32),
            pltpu.VMEM((m, width // 2 + 8, 128), F32),
            pltpu.VMEM((n, width // 2 + 8, 128), F32),
            dma((4, 2)), dma((4, 2)), dma((4,)), dma((4,)),
            dma((m - 1,)), dma((m - 1,)), dma((n - 1,)), dma((n - 1,)),
        ],
        compiler_params=pltpu.CompilerParams(
            collective_id=0, has_side_effects=True, vmem_limit_bytes=65300 * 1024
        ),
    )(
        velocity,
        cotangent,
        block_ids.reshape(1, slots),
        fluid_count,
        fluid_cells.reshape(slots // 2, 128),
        w_in.T,
        w_mid,
        w_out,
    )
    new_field, grad_field, gin_t, gmid, gout = pl.pallas_call(
        hand_on,
        out_shape=outs,
        in_specs=[hbm] * 5,
        out_specs=(hbm,) * 5,
        scratch_shapes=[pltpu.VMEM(out.shape, F32) for out in outs] + [dma((5,)), dma((5,))],
        compiler_params=pltpu.CompilerParams(vmem_limit_bytes=65300 * 1024),
    )(*results)
    return new_field, grad_field, gin_t.T, gmid, gout


def solution(mesh):
    n, m = mesh.shape["gx"], mesh.shape["gy"]
    in_specs = (
        P("gx", "gy", None),
        P("gx", "gy", None),
        P("gx", "gy", None),
        P("gx", "gy"),
        P("gx", "gy", None),
        P(),
        P(),
        P(),
    )
    out_specs = (P("gx", "gy", None), P("gx", "gy", None), P(), P(), P())
    return jax.shard_map(
        functools.partial(body, n, m), mesh=mesh, in_specs=in_specs, out_specs=out_specs, check_vma=False
    )
```
